512 devices in a mesh: gossip: 32 (over z, x_hi, core), fsdp: 16 (over x_lo, y).
Axes of the slice: x: 4 (x_hi: 2, x_lo: 2; x = x_hi * 2 + x_lo), y: 8, z: 8, core: 2. Of those that a mesh axis runs over, the one named last changes fastest.
Arguments:
- patches: bfloat16 [65536, 2048], P(('gossip', 'fsdp')), may hold values from -6 to 6
- query_weight: bfloat16 [32, 2048, 2048], P('gossip', 'fsdp'), may hold values from -6 to 6
- query_grad: bfloat16 [65536, 2048], P(('gossip', 'fsdp')), may hold values from -6 to 6
- step: int32 [1], replicated, may hold values from 0 to 63
Outputs:
- new_weight: bfloat16 [32, 2048, 2048], P('gossip', 'fsdp')
The draws below stay inside these ranges and needn't reach their ends.
All inputs are finite; a program needn't handle non-finite values.
Results may differ from the reference program's by a relative error of at most 0.0056.
Values may be sent and summed in bfloat16 or wider, within the bound.
A program may use at most 64 MiB of HBM per device.

```python
import jax
import jax.numpy as jnp
from jax import lax

DIN = 2048
HEADS = 16
HD = 128
HQ = 2048
REPLICAS = 32
TOKENS = 65536


def level_of(own_key, shape, shards, low, top_value):
    gain, own = 1.0, jax.random.fold_in(own_key, 6)
    for position, shards_of in shards:
        steps = jnp.exp(jax.random.uniform(jax.random.fold_in(own, position), (shards_of,), jnp.float32, low / len(shards), top_value / len(shards)))
        gain = gain * jnp.repeat(steps, shape[position] // shards_of).reshape([-1 if axis == position else 1 for axis in range(len(shape))])
    return gain


def bell_draw(rng, shape, scale, most, split=(), kind=jnp.bfloat16):
    level = level_of(rng, shape, split, -0.22, 0.18) if split else 1.0
    result = jax.random.normal(rng, shape, jnp.float32) * scale * level
    return jnp.minimum(jnp.maximum(result, -most), most).astype(kind)


def setup_inputs(seed: int = 0) -> dict:
    splits = jax.random.split(jax.random.key(seed), 5)
    patches = bell_draw(splits[0], (TOKENS, DIN), 1.0, 6.0, ((0, 512),))
    query_weight = bell_draw(splits[1], (REPLICAS, DIN, HQ), 1.0, 6.0, ((0, 32), (1, 16)))
    query_grad = bell_draw(splits[2], (TOKENS, HQ), 1.0, 6.0, ((0, 512),))
    step = jax.random.randint(splits[3], (1,), 0, 64).astype(jnp.int32)
    return dict(patches=patches, query_weight=query_weight, query_grad=query_grad, step=step)


epsilon = 1e-06

def replica_update(operands):
    patch_rows, weight_rows, grad_rows, learn_rate = operands
    proj_scale = DIN ** (-0.5)
    patch_f = patch_rows.astype(jnp.float32)
    proj = jnp.dot(patch_f, weight_rows.astype(jnp.float32)) * proj_scale
    proj = proj.reshape(proj.shape[0], HEADS, HD)
    inv_rms = lax.rsqrt(lax.optimization_barrier(jnp.mean(proj * proj, axis=-1, keepdims=True)) + epsilon)
    normed = proj * inv_rms
    cotangent = grad_rows.astype(jnp.float32).reshape(normed.shape)
    inner = lax.optimization_barrier(jnp.mean(cotangent * normed, axis=-1, keepdims=True))
    grad_proj = (proj_scale * inv_rms * (cotangent - normed * inner)).astype(jnp.bfloat16)
    grad_proj = lax.optimization_barrier(grad_proj)
    grad_flat = grad_proj.astype(jnp.float32).reshape(patch_rows.shape[0], HEADS * HD)
    weight_grad = jnp.dot(patch_f.T, grad_flat)
    return (weight_rows.astype(jnp.float32) - learn_rate * weight_grad).astype(jnp.bfloat16)

def reference(patches, query_weight, query_grad, step):
    replica_count = query_weight.shape[0]
    patch_groups = patches.reshape(replica_count, -1, DIN)
    grad_groups = query_grad.reshape(replica_count, -1, HEADS * HD)
    learn_rate = 0.5 + (step[0] % 64).astype(jnp.float32) / 64.0
    rates = jnp.full((replica_count,), learn_rate, dtype=jnp.float32)
    updated = lax.map(replica_update, (patch_groups, query_weight, grad_groups, rates))
    hop_size = jnp.left_shift(jnp.int32(1), (step[0] % 4).astype(jnp.int32)) % replica_count
    partner = jnp.roll(updated, hop_size, axis=0)
    mixed = (updated.astype(jnp.float32) + partner.astype(jnp.float32)) * 0.5
    return mixed.astype(jnp.bfloat16)
```

```python
from functools import partial

import jax
import jax.numpy as jnp
from jax import lax
from jax.experimental import pallas as pl
from jax.experimental.pallas import tpu as pltpu
from jax.sharding import PartitionSpec as P

DIN = 2048
HQ = 2048
HD = 128
EPS = 1e-06
MESH = pl.DeviceIdType.MESH

NY = 8
ROWS = 128
FEATS = HQ // NY
HEADS = FEATS // HD
HALF = DIN // 2
TOKS = NY * ROWS
PIECES = 4
PROWS = ROWS // PIECES


def kernel(hop, lr_ref, p_in, w_in, q_in, out, pat, pat_t, wcol, grad_in, normed, scaled_inv, grad, own,
           rs_out, rs_in, upd, upd_in, mixed, loc, w_ss, w_rs, wx_ss, wx_rs, ag_ss, ag_rs, q_ss, q_rs,
           rs_ss, rs_rs, g_ss, g_rs, o_ss, o_rs):
    replicas = lax.axis_size("gossip")
    g, f = lax.axis_index("gossip"), lax.axis_index("fsdp")
    x, y = f // NY, f % NY

    def ring(d):
        return (y + d + NY) % NY

    def along_y(d):
        return (g, x * NY + ring(d))

    across = (g, (1 - x) * NY + y)
    ahead = ((g + hop) % replicas, f)
    behind = ((g + replicas - hop) % replicas, f)

    def copy(src, dst, ss, rs, to):
        return pltpu.make_async_remote_copy(
            src_ref=src, dst_ref=dst, send_sem=ss, recv_sem=rs, device_id=to, device_id_type=MESH)

    def arrived(dst, ss, rs):
        copy(dst, dst, ss, rs, across).wait_recv()

    def block(i, size):
        return pl.ds(pl.multiple_of(i * size, size), size)

    barrier = pltpu.get_barrier_semaphore()
    peers = [along_y(d) for d in range(1, NY)] + [across, ahead, behind]
    for peer in peers:
        pl.semaphore_signal(barrier, inc=1, device_id=peer, device_id_type=MESH)

    cols = block(y, FEATS)
    mine = wcol.at[block(f, ROWS), :]
    local = [
        pltpu.make_async_copy(p_in, pat.at[0], loc.at[0]),
        pltpu.make_async_copy(w_in.at[0, :, cols], mine, loc.at[1]),
    ] + [
        pltpu.make_async_copy(q_in.at[:, block(y * HEADS + h, HD)], grad_in.at[h, 0], loc.at[2 + h])
        for h in range(HEADS)
    ]
    for c in local:
        c.start()
    pl.semaphore_wait(barrier, len(peers))

    sent = []

    def send(*a):
        c = copy(*a)
        c.start()
        sent.append(c)

    for d in (4, 3, 5, 2, 6, 1, 7):
        send(w_in.at[0, :, block(ring(d), FEATS)], mine, w_ss.at[d], w_rs.at[d], along_y(d))
    send(w_in.at[0, :, cols], mine, wx_ss.at[0], wx_rs.at[0], across)

    def piece(ref, p):
        return ref.at[pl.ds(p * PROWS, PROWS), :]

    def on_ring(way, step, p):
        return step < NY // 2 or (p < PIECES // 2) == (way == 0)

    def push(way, step, p):
        slot = NY - step if way == 0 else step
        src = p_in if step == 1 else pat.at[slot + 1 if way == 0 else slot - 1]
        send(piece(src, p), piece(pat.at[slot], p), ag_ss.at[way, step, p], ag_rs.at[way, step, p],
             along_y(1 if way == 0 else -1))

    def pass_on(step):
        for p in range(PIECES):
            for way in range(2):
                if not on_ring(way, step, p):
                    continue
                slot = NY - step if way == 0 else step
                arrived(piece(pat.at[slot], p), ag_ss.at[way, step, p], ag_rs.at[way, step, p])
                if step < NY // 2 and on_ring(way, step + 1, p):
                    push(way, step + 1, p)

    for p in range(PIECES):
        for way in range(2):
            push(way, 1, p)

    for d in (4, 3, 5, 2, 6, 1, 7):
        rows = wcol.at[block(x * NY + ring(-d), ROWS), :]
        arrived(rows, w_ss.at[d], w_rs.at[d])
        send(rows, rows, wx_ss.at[d], wx_rs.at[d], across)

    scale = DIN ** (-0.5)

    def turn(slot):
        pat_t[:, slot * ROWS:(slot + 1) * ROWS] = pat[slot].T

    def project(slot):
        proj = jnp.dot(pat[slot], wcol[...], preferred_element_type=jnp.float32) * scale
        rows = pl.ds(slot * ROWS, ROWS)
        for h in range(HEADS):
            part = proj[:, h * HD:(h + 1) * HD]
            inv = lax.rsqrt(jnp.mean(part * part, axis=-1, keepdims=True) + EPS)
            normed[h, rows, :] = part * inv
            scaled_inv[h, rows, :] = jnp.broadcast_to(scale * inv, part.shape)

    for c in local:
        c.wait()
    pass_on(1)
    for s in (0, 7, 1):
        turn(s)
    pass_on(2)
    for d in range(NY):
        arrived(wcol.at[block((1 - x) * NY + ring(-d), ROWS), :], wx_ss.at[d], wx_rs.at[d])
    for s in (6, 2):
        turn(s)
    for s in (0, 7, 1, 6, 2):
        project(s)
    pass_on(3)
    for h in range(HEADS):
        for d in (4, 3, 5, 2, 6, 1, 7):
            send(q_in.at[:, block(ring(d) * HEADS + h, HD)], grad_in.at[h, NY - d],
                 q_ss.at[h, d], q_rs.at[h, d], along_y(d))
    for s in (5, 3):
        turn(s)
        project(s)
    pass_on(4)
    turn(4)
    project(4)

    rate = lr_ref[0]

    def weight_grad(half, i, h):
        rows = block(half * NY + ring(i + 1), ROWS)
        return jnp.dot(pat_t[rows, :], grad[h], preferred_element_type=jnp.float32)

    def gradient(h):
        for d in range(1, NY):
            arrived(grad_in.at[h, NY - d], q_ss.at[h, d], q_rs.at[h, d])
        cot = grad_in[h].astype(jnp.float32).reshape(TOKS, HD)
        norm = normed[h]
        inner = jnp.mean(cot * norm, axis=-1, keepdims=True)
        grad[h] = (scaled_inv[h] * (cot - norm * inner)).astype(jnp.bfloat16)

        @pl.loop(0, NY)
        def _(i):
            rs_out[h, i] = weight_grad(1 - x, i, h).astype(jnp.bfloat16)
            copy(rs_out.at[h, i], rs_in.at[h, i], rs_ss.at[h, i], rs_rs.at[h, i], across).start()

        @pl.loop(0, NY)
        def _(i):
            own[h, i] = weight_grad(x, i, h)

    def update(h):
        @pl.loop(0, NY)
        def _(i):
            arrived(rs_in.at[h, i], rs_ss.at[h, i], rs_rs.at[h, i])
            total = own[h, i] + rs_in[h, i].astype(jnp.float32)
            old = wcol[block(x * NY + ring(i + 1), ROWS), h * HD:(h + 1) * HD].astype(jnp.float32)
            upd[h, i] = (old - rate * total).astype(jnp.bfloat16)
            copy(upd.at[h, i], upd_in.at[h, i], g_ss.at[h, i], g_rs.at[h, i], ahead).start()

    def place(d, h):
        return out.at[0, :, block(ring(d) * HEADS + h, HD)]

    def mix(h):
        def average(i):
            arrived(upd_in.at[h, i], g_ss.at[h, i], g_rs.at[h, i])
            mean = (upd[h, i].astype(jnp.float32) + upd_in[h, i].astype(jnp.float32)) * 0.5
            mixed[h, i] = mean.astype(jnp.bfloat16)

        @pl.loop(0, NY - 1)
        def _(i):
            average(i)
            copy(mixed.at[h, i], place(0, h), o_ss.at[h, i], o_rs.at[h, i], along_y(i + 1)).start()

        average(NY - 1)
        pltpu.make_async_copy(mixed.at[h, NY - 1], place(0, h), loc.at[h]).start()

    gradient(0)
    update(0)
    gradient(1)
    mix(0)
    update(1)
    mix(1)

    for c in sent:
        c.wait_send()
    for h in range(HEADS):
        pltpu.make_async_copy(mixed.at[h, NY - 1], place(0, h), loc.at[h]).wait()

        @pl.loop(0, NY)
        def _(i):
            copy(rs_out.at[h, i], rs_in.at[h, i], rs_ss.at[h, i], rs_rs.at[h, i], across).wait_send()
            copy(upd.at[h, i], upd_in.at[h, i], g_ss.at[h, i], g_rs.at[h, i], ahead).wait_send()

        @pl.loop(0, NY - 1)
        def _(i):
            copy(mixed.at[h, i], place(0, h), o_ss.at[h, i], o_rs.at[h, i], along_y(i + 1)).wait_send()
            arrived(place(-(i + 1), h), o_ss.at[h, i], o_rs.at[h, i])


def update_weights(exponent, rate, patches, weight, query_grad):
    bf16, f32 = jnp.bfloat16, jnp.float32
    dma = pltpu.SemaphoreType.DMA
    blocks = (HEADS, NY, ROWS, HD)
    return pl.pallas_call(
        partial(kernel, 2 ** exponent),
        out_shape=jax.ShapeDtypeStruct(weight.shape, bf16),
        in_specs=[pl.BlockSpec(memory_space=pltpu.SMEM)] + [pl.BlockSpec(memory_space=pl.ANY)] * 3,
        out_specs=pl.BlockSpec(memory_space=pl.ANY),
        scratch_shapes=[
            pltpu.VMEM((NY, ROWS, DIN), bf16),
            pltpu.VMEM((DIN, TOKS), bf16),
            pltpu.VMEM((DIN, FEATS), bf16),
            pltpu.VMEM(blocks, bf16),
            pltpu.VMEM((HEADS, TOKS, HD), f32),
            pltpu.VMEM((HEADS, TOKS, HD), f32),
            pltpu.VMEM((HEADS, TOKS, HD), bf16),
            pltpu.VMEM(blocks, f32),
            pltpu.VMEM(blocks, bf16),
            pltpu.VMEM(blocks, bf16),
            pltpu.VMEM(blocks, bf16),
            pltpu.VMEM(blocks, bf16),
            pltpu.VMEM(blocks, bf16),
            dma((4,)),
            dma((NY,)), dma((NY,)),
            dma((NY,)), dma((NY,)),
            dma((2, NY // 2 + 1, PIECES)), dma((2, NY // 2 + 1, PIECES)),
            dma((HEADS, NY)), dma((HEADS, NY)),
            dma((HEADS, NY)), dma((HEADS, NY)),
            dma((HEADS, NY)), dma((HEADS, NY)),
            dma((HEADS, NY)), dma((HEADS, NY)),
        ],
        compiler_params=pltpu.CompilerParams(
            collective_id=exponent, has_side_effects=True, vmem_limit_bytes=40 << 20),
        cost_estimate=pl.CostEstimate(
            flops=8 * TOKS * DIN * FEATS, bytes_accessed=8 << 20, transcendentals=TOKS * HEADS),
        name=f"replica_update_hop{2 ** exponent}",
    )(rate, patches, weight, query_grad)


def on_device(patches, query_weight, query_grad, step):
    rate = 0.5 + (step % 64).astype(jnp.float32) / 64.0
    branches = [partial(update_weights, exponent) for exponent in range(4)]
    return lax.switch(step[0] % 4, branches, rate, patches, query_weight, query_grad)


def solution(mesh):
    in_specs = (
        P(("gossip", "fsdp"), None),
        P("gossip", "fsdp", None),
        P(("gossip", "fsdp"), None),
        P(),
    )
    out_specs = P("gossip", "fsdp", None)
    return jax.shard_map(
        on_device, mesh=mesh, in_specs=in_specs, out_specs=out_specs, check_vma=False
    )
```

```python
from functools import partial

import jax
import jax.numpy as jnp
from jax import lax
from jax.experimental import pallas as pl
from jax.experimental.pallas import tpu as pltpu
from jax.sharding import PartitionSpec as P

DIN = 2048
HQ = 2048
HD = 128
EPS = 1e-06
MESH = pl.DeviceIdType.MESH

NY = 8
ROWS = 128
HALF = DIN // 2
FEATS = HQ // (NY // 2)
HEADS = FEATS // HD
SLOTS = 4
TOKS = 2 * SLOTS * ROWS
PIECES = 4
PROWS = 2 * ROWS // PIECES
OTHER_FIRST = (2, 3, 0, 1)


def kernel(hop, lr_ref, p_in, w_in, q_in, out, pat, pat_t, wcol, part, part_out, part_in, grad_in, normed,
           scaled_inv, grad, own, rs_out, rs_in, upd, upd_in, mixed, loc, pre_ss, pre_rs, w_ss, w_rs, ag_ss, ag_rs,
           pt_ss, pt_rs, q_ss, q_rs, x_ss, x_rs, rs_ss, rs_rs, g_ss, g_rs, o_ss, o_rs):
    replicas = lax.axis_size("gossip")
    g, f = lax.axis_index("gossip"), lax.axis_index("fsdp")
    x, y = f // NY, f % NY
    sign = 1 - 2 * (y % 2)

    def ring(k):
        return (y + k * sign + NY) % NY

    def node(k):
        return (g, x * NY + ring(k))

    def pair(k):
        return ring(k) // 2

    across = (g, (1 - x) * NY + y)
    ahead = ((g + hop) % replicas, f)
    behind = ((g + replicas - hop) % replicas, f)

    def copy(src, dst, ss, rs, to):
        return pltpu.make_async_remote_copy(
            src_ref=src, dst_ref=dst, send_sem=ss, recv_sem=rs, device_id=to, device_id_type=MESH)

    def arrived(dst, ss, rs):
        copy(dst, dst, ss, rs, across).wait_recv()

    def block(i, size):
        return pl.ds(pl.multiple_of(i * size, size), size)

    barrier = pltpu.get_barrier_semaphore()
    peers = [node(k) for k in (1, -1, 2, -2, -3)] + [across, ahead, behind]
    for peer in peers:
        pl.semaphore_signal(barrier, inc=1, device_id=peer, device_id_type=MESH)

    def head_cols(k, h):
        return block(pair(k) * HEADS + h, HD)

    def weight_rows(k):
        return wcol.at[block(ring(k), ROWS), :]

    local = [
        pltpu.make_async_copy(p_in.at[:, block(x, HALF)], pat.at[0, 0], loc.at[0]),
        pltpu.make_async_copy(w_in.at[0, :, block(pair(0), FEATS)], weight_rows(0), loc.at[1]),
    ] + [
        pltpu.make_async_copy(q_in.at[:, head_cols(0, h)], grad_in.at[h, 0], loc.at[2 + h]) for h in range(HEADS)
    ]
    for c in local:
        c.start()
    pl.semaphore_wait(barrier, len(peers))

    sent = []

    def send(*a):
        c = copy(*a)
        c.start()
        sent.append(c)

    for p in range(PIECES // 2):
        rows = pl.ds(p * PROWS, PROWS)
        send(p_in.at[rows, block(1 - x, HALF)], pat.at[0, 1, rows, :], pre_ss.at[p], pre_rs.at[p], across)

    def piece(slot, p):
        return pat.at[slot, p // 2, pl.ds(p % 2 * PROWS, PROWS), :]

    def push(src, slot, p, to):
        send(src, piece(slot, p), ag_ss.at[slot, p], ag_rs.at[slot, p], node(to))

    def landed(slot, p):
        arrived(piece(slot, p), ag_ss.at[slot, p], ag_rs.at[slot, p])

    for k, sem in ((-3, 3), (2, 2), (-1, 1), (1, 0)):
        send(w_in.at[0, :, block(pair(k), FEATS)], weight_rows(0), w_ss.at[sem], w_rs.at[sem], node(k))
    for p in OTHER_FIRST:
        src = piece(0, p)
        if p < PIECES // 2:
            src = p_in.at[pl.ds(p * PROWS, PROWS), block(x, HALF)]
        else:
            q = p - PIECES // 2
            arrived(src, pre_ss.at[q], pre_rs.at[q])
        push(src, 1, p, -1)
        push(src, 4, p, 1)
    for k in (1, 2, 3):
        arrived(weight_rows(-k), w_ss.at[k], w_rs.at[k])
        send(weight_rows(-k), weight_rows(-k), w_ss.at[3 + k], w_rs.at[3 + k], node(1))

    def send_grads(h):
        for k, sem in ((-3, 3), (2, 2), (-1, 1)):
            send(q_in.at[:, head_cols(k, h)], grad_in.at[h, sem], q_ss.at[h, sem], q_rs.at[h, sem], node(k))

    scale = DIN ** (-0.5)

    def turn(slot):
        for c in range(2):
            at = (c * SLOTS + slot) * ROWS
            pat_t[:, at:at + ROWS] = pat[slot, c].T

    def product(slot, c):
        return jnp.dot(pat[slot, c], wcol[...], preferred_element_type=jnp.float32)

    def project_other(slot):
        part_out[slot] = product(slot, 1).astype(jnp.bfloat16)
        send(part_out.at[slot], part_in.at[slot], pt_ss.at[slot], pt_rs.at[slot], across)

    def project_own(slot):
        part[slot] = product(slot, 0)

    def project(slot):
        project_other(slot)
        project_own(slot)

    def finish(slot):
        arrived(part_in.at[slot], pt_ss.at[slot], pt_rs.at[slot])
        proj = (part[slot] + part_in[slot].astype(jnp.float32)) * scale
        rows = pl.ds(slot * ROWS, ROWS)
        for h in range(HEADS):
            own_part = proj[:, h * HD:(h + 1) * HD]
            inv = lax.rsqrt(jnp.mean(own_part * own_part, axis=-1, keepdims=True) + EPS)
            normed[h, rows, :] = own_part * inv
            scaled_inv[h, rows, :] = jnp.broadcast_to(scale * inv, own_part.shape)

    for c in local:
        c.wait()
    turn(0)
    for p in OTHER_FIRST:
        landed(1, p)
        push(piece(1, p), 5, p, 1)
        landed(4, p)
        push(piece(4, p), 2, p, -1)
    turn(1)
    arrived(weight_rows(1), w_ss.at[0], w_rs.at[0])
    for k in (1, 2, 3):
        arrived(weight_rows(k + 1), w_ss.at[3 + k], w_rs.at[3 + k])
    project(0)
    project(1)
    for p in OTHER_FIRST:
        landed(5, p)
        push(piece(5, p), 3, p, -1)
        landed(2, p)
    turn(2)
    project(2)
    finish(0)
    finish(1)
    early = len(sent)
    for p in OTHER_FIRST:
        landed(3, p)
        for h in GRADS_AT[p]:
            send_grads(h)
        if p == OTHER_FIRST[1]:
            project_other(3)
            for c in sent[:early]:
                c.wait_send()
            finish(2)
    project_own(3)
    turn(3)
    finish(3)

    rate = lr_ref[0]

    def grad_across(h, slot):
        return copy(grad.at[h, pl.ds(slot * ROWS, ROWS), :], grad.at[h, pl.ds((SLOTS + slot) * ROWS, ROWS), :],
                    x_ss.at[h, slot], x_rs.at[h, slot], across)

    def to_pair(h, i):
        return copy(rs_out.at[h, i], rs_in.at[h, i], rs_ss.at[h, i], rs_rs.at[h, i], node(1))

    def to_partner(h, i):
        return copy(upd.at[h, i], upd_in.at[h, i], g_ss.at[h, i], g_rs.at[h, i], ahead)

    def to_owner(h, i):
        place = out.at[0, :, head_cols(0, h)]
        if i == 0:
            return pltpu.make_async_copy(mixed.at[h, i], place, loc.at[h])
        return copy(mixed.at[h, i], place, o_ss.at[h, i], o_rs.at[h, i], node(-i))

    def gradient(h):
        for slot in range(SLOTS):
            if slot:
                arrived(grad_in.at[h, slot], q_ss.at[h, slot], q_rs.at[h, slot])
            rows = pl.ds(slot * ROWS, ROWS)
            cot = grad_in[h, slot].astype(jnp.float32)
            norm = normed[h, rows, :]
            inner = jnp.mean(cot * norm, axis=-1, keepdims=True)
            grad[h, rows, :] = (scaled_inv[h, rows, :] * (cot - norm * inner)).astype(jnp.bfloat16)
            grad_across(h, slot).start()

    def weight_grad(k, h):
        return jnp.dot(pat_t[block(ring(k), ROWS), :], grad[h], preferred_element_type=jnp.float32)

    def sums(h):
        for slot in range(SLOTS):
            arrived(grad.at[h, pl.ds((SLOTS + slot) * ROWS, ROWS), :], x_ss.at[h, slot], x_rs.at[h, slot])
        for i in range(SLOTS):
            rs_out[h, i] = weight_grad(i + 1, h).astype(jnp.bfloat16)
            to_pair(h, i).start()
        for i in range(SLOTS):
            own[h, i] = weight_grad(-i, h)

    def update(h):
        for i in range(SLOTS):
            arrived(rs_in.at[h, i], rs_ss.at[h, i], rs_rs.at[h, i])
            total = own[h, i] + rs_in[h, i].astype(jnp.float32)
            old = wcol[block(ring(-i), ROWS), h * HD:(h + 1) * HD].astype(jnp.float32)
            upd[h, i] = (old - rate * total).astype(jnp.bfloat16)
            to_partner(h, i).start()

    def mix(h):
        for i in range(SLOTS):
            arrived(upd_in.at[h, i], g_ss.at[h, i], g_rs.at[h, i])
            mean = (upd[h, i].astype(jnp.float32) + upd_in[h, i].astype(jnp.float32)) * 0.5
            mixed[h, i] = mean.astype(jnp.bfloat16)
            to_owner(h, i).start()

    for step, h in STEPS:
        (gradient, sums, update, mix)[step](h)

    for c in sent[early:]:
        c.wait_send()
    for h in range(HEADS):
        for i in range(SLOTS):
            grad_across(h, i).wait_send()
            to_pair(h, i).wait_send()
            to_partner(h, i).wait_send()
            if i == 0:
                to_owner(h, i).wait()
            else:
                to_owner(h, i).wait_send()
                source = (None, -1, 2, -3)[i]
                arrived(out.at[0, :, head_cols(source, h)], o_ss.at[h, i], o_rs.at[h, i])


STEPS = ((0, 0), (0, 1), (1, 0), (0, 2), (1, 1), (2, 0), (0, 3), (1, 2), (2, 1), (3, 0), (1, 3), (2, 2), (3, 1),
         (2, 3), (3, 2), (3, 3))
GRADS_AT = ((1,2), (3,), (0,), ())


def update_weights(exponent, rate, patches, weight, query_grad):
    bf16, f32 = jnp.bfloat16, jnp.float32
    dma = pltpu.SemaphoreType.DMA
    blocks = (HEADS, SLOTS, ROWS, HD)
    return pl.pallas_call(
        partial(kernel, 2 ** exponent),
        out_shape=jax.ShapeDtypeStruct(weight.shape, bf16),
        in_specs=[pl.BlockSpec(memory_space=pltpu.SMEM)] + [pl.BlockSpec(memory_space=pl.ANY)] * 3,
        out_specs=pl.BlockSpec(memory_space=pl.ANY),
        scratch_shapes=[
            pltpu.VMEM((SLOTS + 2, 2, ROWS, HALF), bf16),
            pltpu.VMEM((HALF, TOKS), bf16),
            pltpu.VMEM((HALF, FEATS), bf16),
            pltpu.VMEM((SLOTS, ROWS, FEATS), f32),
            pltpu.VMEM((SLOTS, ROWS, FEATS), bf16),
            pltpu.VMEM((SLOTS, ROWS, FEATS), bf16),
            pltpu.VMEM(blocks, bf16),
            pltpu.VMEM((HEADS, SLOTS * ROWS, HD), f32),
            pltpu.VMEM((HEADS, SLOTS * ROWS, HD), f32),
            pltpu.VMEM((HEADS, TOKS, HD), bf16),
            pltpu.VMEM(blocks, f32),
            pltpu.VMEM(blocks, bf16),
            pltpu.VMEM(blocks, bf16),
            pltpu.VMEM(blocks, bf16),
            pltpu.VMEM(blocks, bf16),
            pltpu.VMEM(blocks, bf16),
            dma((2 + HEADS,)),
            dma((PIECES // 2,)), dma((PIECES // 2,)),
            dma((7,)), dma((7,)),
            dma((SLOTS + 2, PIECES)), dma((SLOTS + 2, PIECES)),
            dma((SLOTS,)), dma((SLOTS,)),
            dma((HEADS, SLOTS)), dma((HEADS, SLOTS)),
            dma((HEADS, SLOTS)), dma((HEADS, SLOTS)),
            dma((HEADS, SLOTS)), dma((HEADS, SLOTS)),
            dma((HEADS, SLOTS)), dma((HEADS, SLOTS)),
            dma((HEADS, SLOTS)), dma((HEADS, SLOTS)),
        ],
        compiler_params=pltpu.CompilerParams(
            collective_id=exponent, has_side_effects=True, vmem_limit_bytes=40 << 20),
        cost_estimate=pl.CostEstimate(
            flops=8 * TOKS * HALF * FEATS, bytes_accessed=8 << 20, transcendentals=SLOTS * ROWS * HEADS),
        name=f"replica_update_hop{2 ** exponent}",
    )(rate, patches, weight, query_grad)


def on_device(patches, query_weight, query_grad, step):
    rate = 0.5 + (step % 64).astype(jnp.float32) / 64.0
    branches = [partial(update_weights, exponent) for exponent in range(4)]
    return lax.switch(step[0] % 4, branches, rate, patches, query_weight, query_grad)


def solution(mesh):
    in_specs = (
        P(("gossip", "fsdp"), None),
        P("gossip", "fsdp", None),
        P(("gossip", "fsdp"), None),
        P(),
    )
    out_specs = P("gossip", "fsdp", None)
    return jax.shard_map(
        on_device, mesh=mesh, in_specs=in_specs, out_specs=out_specs, check_vma=False
    )
```

```python
from functools import partial

import jax
import jax.numpy as jnp
from jax import lax
from jax.experimental import pallas as pl
from jax.experimental.pallas import tpu as pltpu
from jax.sharding import PartitionSpec as P

DIN = 2048
HQ = 2048
HD = 128
EPS = 1e-06
MESH = pl.DeviceIdType.MESH

NY = 8
ROWS = 128
HALF = DIN // 2
FEATS = HQ // (NY // 2)
HEADS = FEATS // HD
SLOTS = 4
TOKS = 2 * SLOTS * ROWS
PIECES = 4
PROWS = 2 * ROWS // PIECES
OTHER_FIRST = (2, 3, 0, 1)


def kernel(hop, lr_ref, p_in, w_in, q_in, out, pat, pat_t, wcol, part, part_out, part_in, grad_in, normed,
           scaled_inv, grad, own, rs_out, rs_in, upd, upd_in, mixed, loc, pre_ss, pre_rs, w_ss, w_rs, ag_ss, ag_rs,
           pt_ss, pt_rs, q_ss, q_rs, x_ss, x_rs, rs_ss, rs_rs, g_ss, g_rs, o_ss, o_rs):
    replicas = lax.axis_size("gossip")
    g, f = lax.axis_index("gossip"), lax.axis_index("fsdp")
    x, y = f // NY, f % NY
    sign = 1 - 2 * (y % 2)

    def ring(k):
        return (y + k * sign + NY) % NY

    def node(k):
        return (g, x * NY + ring(k))

    def pair(k):
        return ring(k) // 2

    across = (g, (1 - x) * NY + y)
    ahead = ((g + hop) % replicas, f)
    behind = ((g + replicas - hop) % replicas, f)

    def copy(src, dst, ss, rs, to):
        return pltpu.make_async_remote_copy(
            src_ref=src, dst_ref=dst, send_sem=ss, recv_sem=rs, device_id=to, device_id_type=MESH)

    def arrived(dst, ss, rs):
        copy(dst, dst, ss, rs, across).wait_recv()

    def block(i, size):
        return pl.ds(pl.multiple_of(i * size, size), size)

    barrier = pltpu.get_barrier_semaphore()
    peers = [node(k) for k in (1, -1, 2, -2, -3)] + [across, ahead, behind]
    for peer in peers:
        pl.semaphore_signal(barrier, inc=1, device_id=peer, device_id_type=MESH)

    def head_cols(k, h):
        return block(pair(k) * HEADS + h, HD)

    def weight_rows(k):
        return wcol.at[block(ring(k), ROWS), :]

    local = [
        pltpu.make_async_copy(p_in.at[:, block(x, HALF)], pat.at[0, 0], loc.at[0]),
        pltpu.make_async_copy(w_in.at[0, :, block(pair(0), FEATS)], weight_rows(0), loc.at[1]),
    ] + [
        pltpu.make_async_copy(q_in.at[:, head_cols(0, h)], grad_in.at[h, 0], loc.at[2 + h]) for h in range(HEADS)
    ]
    for c in local:
        c.start()
    pl.semaphore_wait(barrier, len(peers))

    sent = []

    def send(*a):
        c = copy(*a)
        c.start()
        sent.append(c)

    for p in range(PIECES // 2):
        rows = pl.ds(p * PROWS, PROWS)
        send(p_in.at[rows, block(1 - x, HALF)], pat.at[0, 1, rows, :], pre_ss.at[p], pre_rs.at[p], across)

    def piece(slot, p):
        return pat.at[slot, p // 2, pl.ds(p % 2 * PROWS, PROWS), :]

    def push(src, slot, p, to):
        send(src, piece(slot, p), ag_ss.at[slot, p], ag_rs.at[slot, p], node(to))

    def landed(slot, p):
        arrived(piece(slot, p), ag_ss.at[slot, p], ag_rs.at[slot, p])

    for k, sem in ((-3, 3), (2, 2), (-1, 1), (1, 0)):
        send(w_in.at[0, :, block(pair(k), FEATS)], weight_rows(0), w_ss.at[sem], w_rs.at[sem], node(k))
    for p in OTHER_FIRST:
        src = piece(0, p)
        if p < PIECES // 2:
            src = p_in.at[pl.ds(p * PROWS, PROWS), block(x, HALF)]
        else:
            q = p - PIECES // 2
            arrived(src, pre_ss.at[q], pre_rs.at[q])
        push(src, 1, p, -1)
        push(src, 4, p, 1)
    for k in (1, 2, 3):
        arrived(weight_rows(-k), w_ss.at[k], w_rs.at[k])
        send(weight_rows(-k), weight_rows(-k), w_ss.at[3 + k], w_rs.at[3 + k], node(1))

    def send_grads(h):
        for k, sem in ((-3, 3), (2, 2), (-1, 1)):
            send(q_in.at[:, head_cols(k, h)], grad_in.at[h, sem], q_ss.at[h, sem], q_rs.at[h, sem], node(k))

    scale = DIN ** (-0.5)

    def turn(slot):
        for c in range(2):
            at = (c * SLOTS + slot) * ROWS
            pat_t[:, at:at + ROWS] = pat[slot, c].T

    def product(slot, c):
        return jnp.dot(pat[slot, c], wcol[...], preferred_element_type=jnp.float32)

    def project_other(slot):
        part_out[slot] = product(slot, 1).astype(jnp.bfloat16)
        send(part_out.at[slot], part_in.at[slot], pt_ss.at[slot], pt_rs.at[slot], across)

    def project_own(slot):
        part[slot] = product(slot, 0)

    def project(slot):
        project_other(slot)
        project_own(slot)

    def finish(slot):
        arrived(part_in.at[slot], pt_ss.at[slot], pt_rs.at[slot])
        proj = (part[slot] + part_in[slot].astype(jnp.float32)) * scale
        rows = pl.ds(slot * ROWS, ROWS)
        for h in range(HEADS):
            own_part = proj[:, h * HD:(h + 1) * HD]
            inv = lax.rsqrt(jnp.mean(own_part * own_part, axis=-1, keepdims=True) + EPS)
            normed[h, rows, :] = own_part * inv
            scaled_inv[h, rows, :] = jnp.broadcast_to(scale * inv, own_part.shape)

    for c in local:
        c.wait()
    turn(0)
    for p in OTHER_FIRST:
        landed(4, p)
        push(piece(4, p), 2, p, -1)
        landed(1, p)
        push(piece(1, p), 5, p, 1)
    turn(1)
    arrived(weight_rows(1), w_ss.at[0], w_rs.at[0])
    for k in (1, 2, 3):
        arrived(weight_rows(k + 1), w_ss.at[3 + k], w_rs.at[3 + k])
    project(0)
    project(1)
    for p in OTHER_FIRST:
        landed(5, p)
        push(piece(5, p), 3, p, -1)
        landed(2, p)
    turn(2)
    project(2)
    finish(0)
    finish(1)
    early = len(sent)
    for p in OTHER_FIRST:
        landed(3, p)
        for h in GRADS_AT[p]:
            send_grads(h)
        if p == OTHER_FIRST[1]:
            project_other(3)
            for c in sent[:early]:
                c.wait_send()
            finish(2)
    project_own(3)
    turn(3)
    finish(3)

    rate = lr_ref[0]

    def grad_across(h, slot):
        return copy(grad.at[h, pl.ds(slot * ROWS, ROWS), :], grad.at[h, pl.ds((SLOTS + slot) * ROWS, ROWS), :],
                    x_ss.at[h, slot], x_rs.at[h, slot], across)

    def to_pair(h, i):
        return copy(rs_out.at[h, i], rs_in.at[h, i], rs_ss.at[h, i], rs_rs.at[h, i], node(1))

    def to_partner(h, i):
        return copy(upd.at[h, i], upd_in.at[h, i], g_ss.at[h, i], g_rs.at[h, i], ahead)

    def to_owner(h, i):
        place = out.at[0, :, head_cols(0, h)]
        if i == 0:
            return pltpu.make_async_copy(mixed.at[h, i], place, loc.at[h])
        return copy(mixed.at[h, i], place, o_ss.at[h, i], o_rs.at[h, i], node(-i))

    def gradient(h):
        for slot in range(SLOTS):
            if slot:
                arrived(grad_in.at[h, slot], q_ss.at[h, slot], q_rs.at[h, slot])
            rows = pl.ds(slot * ROWS, ROWS)
            cot = grad_in[h, slot].astype(jnp.float32)
            norm = normed[h, rows, :]
            inner = jnp.mean(cot * norm, axis=-1, keepdims=True)
            grad[h, rows, :] = (scaled_inv[h, rows, :] * (cot - norm * inner)).astype(jnp.bfloat16)
            grad_across(h, slot).start()

    def weight_grad(k, h):
        return jnp.dot(pat_t[block(ring(k), ROWS), :], grad[h], preferred_element_type=jnp.float32)

    def sums(h):
        for slot in range(SLOTS):
            arrived(grad.at[h, pl.ds((SLOTS + slot) * ROWS, ROWS), :], x_ss.at[h, slot], x_rs.at[h, slot])
        for i in range(SLOTS):
            rs_out[h, i] = weight_grad(i + 1, h).astype(jnp.bfloat16)
            to_pair(h, i).start()
        for i in range(SLOTS):
            own[h, i] = weight_grad(-i, h)

    def update(h):
        for i in range(SLOTS):
            arrived(rs_in.at[h, i], rs_ss.at[h, i], rs_rs.at[h, i])
            total = own[h, i] + rs_in[h, i].astype(jnp.float32)
            old = wcol[block(ring(-i), ROWS), h * HD:(h + 1) * HD].astype(jnp.float32)
            upd[h, i] = (old - rate * total).astype(jnp.bfloat16)
            to_partner(h, i).start()

    def mix(h):
        for i in range(SLOTS):
            arrived(upd_in.at[h, i], g_ss.at[h, i], g_rs.at[h, i])
            mean = (upd[h, i].astype(jnp.float32) + upd_in[h, i].astype(jnp.float32)) * 0.5
            mixed[h, i] = mean.astype(jnp.bfloat16)
            to_owner(h, i).start()

    for step, h in STEPS:
        (gradient, sums, update, mix)[step](h)

    for c in sent[early:]:
        c.wait_send()
    for h in range(HEADS):
        for i in range(SLOTS):
            grad_across(h, i).wait_send()
            to_pair(h, i).wait_send()
            to_partner(h, i).wait_send()
            if i == 0:
                to_owner(h, i).wait()
            else:
                to_owner(h, i).wait_send()
                source = (None, -1, 2, -3)[i]
                arrived(out.at[0, :, head_cols(source, h)], o_ss.at[h, i], o_rs.at[h, i])


STEPS = ((0, 0), (0, 1), (1, 0), (0, 2), (1, 1), (2, 0), (0, 3), (1, 2), (2, 1), (3, 0), (1, 3), (2, 2), (3, 1),
         (2, 3), (3, 2), (3, 3))
GRADS_AT = ((1,2), (3,), (0,), ())


def update_weights(exponent, rate, patches, weight, query_grad):
    bf16, f32 = jnp.bfloat16, jnp.float32
    dma = pltpu.SemaphoreType.DMA
    blocks = (HEADS, SLOTS, ROWS, HD)
    return pl.pallas_call(
        partial(kernel, 2 ** exponent),
        out_shape=jax.ShapeDtypeStruct(weight.shape, bf16),
        in_specs=[pl.BlockSpec(memory_space=pltpu.SMEM)] + [pl.BlockSpec(memory_space=pl.ANY)] * 3,
        out_specs=pl.BlockSpec(memory_space=pl.ANY),
        scratch_shapes=[
            pltpu.VMEM((SLOTS + 2, 2, ROWS, HALF), bf16),
            pltpu.VMEM((HALF, TOKS), bf16),
            pltpu.VMEM((HALF, FEATS), bf16),
            pltpu.VMEM((SLOTS, ROWS, FEATS), f32),
            pltpu.VMEM((SLOTS, ROWS, FEATS), bf16),
            pltpu.VMEM((SLOTS, ROWS, FEATS), bf16),
            pltpu.VMEM(blocks, bf16),
            pltpu.VMEM((HEADS, SLOTS * ROWS, HD), f32),
            pltpu.VMEM((HEADS, SLOTS * ROWS, HD), f32),
            pltpu.VMEM((HEADS, TOKS, HD), bf16),
            pltpu.VMEM(blocks, f32),
            pltpu.VMEM(blocks, bf16),
            pltpu.VMEM(blocks, bf16),
            pltpu.VMEM(blocks, bf16),
            pltpu.VMEM(blocks, bf16),
            pltpu.VMEM(blocks, bf16),
            dma((2 + HEADS,)),
            dma((PIECES // 2,)), dma((PIECES // 2,)),
            dma((7,)), dma((7,)),
            dma((SLOTS + 2, PIECES)), dma((SLOTS + 2, PIECES)),
            dma((SLOTS,)), dma((SLOTS,)),
            dma((HEADS, SLOTS)), dma((HEADS, SLOTS)),
            dma((HEADS, SLOTS)), dma((HEADS, SLOTS)),
            dma((HEADS, SLOTS)), dma((HEADS, SLOTS)),
            dma((HEADS, SLOTS)), dma((HEADS, SLOTS)),
            dma((HEADS, SLOTS)), dma((HEADS, SLOTS)),
        ],
        compiler_params=pltpu.CompilerParams(
            collective_id=exponent, has_side_effects=True, vmem_limit_bytes=40 << 20),
        cost_estimate=pl.CostEstimate(
            flops=8 * TOKS * HALF * FEATS, bytes_accessed=8 << 20, transcendentals=SLOTS * ROWS * HEADS),
        name=f"replica_update_hop{2 ** exponent}",
    )(rate, patches, weight, query_grad)


def on_device(patches, query_weight, query_grad, step):
    rate = 0.5 + (step % 64).astype(jnp.float32) / 64.0
    branches = [partial(update_weights, exponent) for exponent in range(4)]
    return lax.switch(step[0] % 4, branches, rate, patches, query_weight, query_grad)


def solution(mesh):
    in_specs = (
        P(("gossip", "fsdp"), None),
        P("gossip", "fsdp", None),
        P(("gossip", "fsdp"), None),
        P(),
    )
    out_specs = P("gossip", "fsdp", None)
    return jax.shard_map(
        on_device, mesh=mesh, in_specs=in_specs, out_specs=out_specs, check_vma=False
    )
```
